256 devices in a mesh: section: 8 (over z), seq: 32 (over x, y, core).
Axes of the slice: x: 4, y: 4, z: 8, core: 2. Of those that a mesh axis runs over, the one named last changes fastest.
Arguments:
- patch_qkv: bfloat16 [16, 2, 32, 3, 16384], P('section', None, None, None, 'seq'), may hold values from -12 to 12
- kv_cache: bfloat16 [16, 2, 32, 2, 65536], P('section', None, 'seq'), may hold values from -12 to 12
- text_kv: bfloat16 [16, 2, 32, 2, 21312], P('section', None, 'seq'), may hold values from -12 to 12
- entering: bfloat16 [8, 2, 32, 16384], P('section', None, None, 'seq'), may hold values from -6 to 6
- gates: float32 [16, 2, 32], P('section'), may hold values from 0.3 to 3
- block_split: int32 [8], P('section'), may hold values from 1 to 2
- patch_index: int32 [8], P('section'), may hold values from 0 to 3
Outputs:
- new_cache: bfloat16 [16, 2, 32, 2, 65536], P('section', None, 'seq')
- attended: bfloat16 [16, 2, 32, 16384], P('section', None, 'seq')
- handed: bfloat16 [8, 2, 32, 16384], P('section', None, None, 'seq')
The draws below stay inside these ranges and needn't reach their ends.
All inputs are finite; a program needn't handle non-finite values.
Results may differ from the reference program's by a relative error of at most 0.006.
Values may be sent and summed in bfloat16 or wider, within the bound.
A program may use at most 64 MiB of HBM per device.

```python
import math
import jax
import jax.numpy as jnp
from jax import lax

HD = 64
HEADS = 32
PTOK = 256
PATCHES = 4
IMG = 1024
TXT = 333
GUIDE = 2
LAYERS = 2
N_SECTION = 8


def spread_normal(key, full_shape, token_dim):
    base_draw = jax.random.normal(key, full_shape, jnp.float32)
    token_shape = [1] * len(full_shape)
    token_shape[token_dim] = full_shape[token_dim]
    channel_shape = [1] * len(full_shape)
    channel_shape[-1] = full_shape[-1]
    row_scale = jnp.exp(jax.random.uniform(jax.random.fold_in(key, 1), tuple(token_shape), jnp.float32, math.log(0.3), math.log(3.0)))
    column_scale = jnp.exp(jax.random.uniform(jax.random.fold_in(key, 2), tuple(channel_shape), jnp.float32, math.log(0.6), math.log(1.6)))
    return base_draw * row_scale * column_scale


def draw_patch_qkv(key, part):
    key = jax.random.fold_in(key, 11)
    full_shape = (N_SECTION * LAYERS, GUIDE, HEADS, 3, PTOK, HD)
    drawn = spread_normal(key, full_shape, 4)
    return jnp.clip(drawn, -12.0, 12.0).reshape(N_SECTION * LAYERS, GUIDE, HEADS, 3, PTOK * HD).astype(jnp.bfloat16)


def draw_kv_cache(key, part):
    key = jax.random.fold_in(key, 13)
    drawn = spread_normal(key, (N_SECTION * LAYERS, GUIDE, HEADS, 2, IMG, HD), 4)
    return jnp.clip(drawn, -12.0, 12.0).reshape(N_SECTION * LAYERS, GUIDE, HEADS, 2, IMG * HD).astype(jnp.bfloat16)


def draw_text_kv(key, part):
    key = jax.random.fold_in(key, 17)
    drawn = spread_normal(key, (N_SECTION * LAYERS, GUIDE, HEADS, 2, TXT, HD), 4)
    return jnp.clip(drawn, -12.0, 12.0).reshape(N_SECTION * LAYERS, GUIDE, HEADS, 2, TXT * HD).astype(jnp.bfloat16)


def with_ends(entries, rng, low, largest):
    shape = entries.shape
    spot = [jax.random.randint(jax.random.fold_in(rng, axis), (), 0, shape[axis]) for axis in range(len(shape))]
    entries = entries.at[tuple(spot)].set(low)
    longest = shape.index(max(shape))
    spot[longest] = (spot[longest] + 1) % shape[longest]
    return entries.at[tuple(spot)].set(largest)


def block_scale(own_key, extent, cuts, smallest, high):
    def one(dim, blocks):
        steps = jax.random.uniform(jax.random.fold_in(jax.random.fold_in(own_key, 6), dim), (blocks,), jnp.float32, smallest / len(cuts), high / len(cuts))
        return jnp.repeat(jnp.exp(steps), extent[dim] // blocks).reshape((-1,) + (1,) * (len(extent) - dim - 1))

    loudness = one(*cuts[0])
    for cut in cuts[1:]:
        loudness = loudness * one(*cut)
    return loudness


def bell_draw(own_key, extent, width, most, split=(), held_as=jnp.bfloat16):
    values = jax.random.normal(own_key, extent, jnp.float32) * width
    if len(split) > 0:
        values = block_scale(own_key, extent, split, -0.22, 0.18) * values
    return jnp.clip(values, min=-most, max=most).astype(held_as)


def setup_inputs(seed: int = 0) -> dict:
    arg_keys = jax.random.split(jax.random.key(seed), 8)
    patch_qkv = draw_patch_qkv(jax.random.fold_in(arg_keys[7], 71), 0)
    kv_cache = draw_kv_cache(jax.random.fold_in(arg_keys[7], 71), 0)
    text_kv = draw_text_kv(jax.random.fold_in(arg_keys[7], 71), 0)
    entering = bell_draw(arg_keys[3], (N_SECTION, GUIDE, HEADS, PTOK * HD), 1.0, 6.0, ((0, 8), (3, 32)))
    gates = jnp.clip(jnp.exp(math.log(3.0) - 2.3025851 * jax.random.uniform(arg_keys[4], (N_SECTION * LAYERS, GUIDE, HEADS), jnp.float32) ** block_scale(arg_keys[4], (N_SECTION * LAYERS, GUIDE, HEADS), ((0, 8),), -0.2, 0.2)), 0.3, 3.0)
    block_split = with_ends(jax.random.randint(arg_keys[5], (N_SECTION,), 1, LAYERS + 1), jax.random.fold_in(arg_keys[5], 1), 1, LAYERS).astype(jnp.int32)
    patch_index = with_ends(jax.random.randint(arg_keys[6], (N_SECTION,), 0, PATCHES), jax.random.fold_in(arg_keys[6], 1), 0, PATCHES - 1).astype(jnp.int32)
    return dict(patch_qkv=patch_qkv, kv_cache=kv_cache, text_kv=text_kv, entering=entering, gates=gates, block_split=block_split, patch_index=patch_index)


def attend_blocks(queries, key_rows, value_rows):
    row_count = queries.shape[2]
    block_rows = min(row_count, 512)
    pieces = queries.reshape(queries.shape[0], queries.shape[1], row_count // block_rows, block_rows, queries.shape[3])
    pieces = jnp.moveaxis(pieces, 2, 0)
    factor = queries.shape[3] ** -0.5

    def attend_block(query_part):
        scores = jnp.einsum("ghqd,ghkd->ghqk", query_part.astype(jnp.float32), key_rows.astype(jnp.float32)) * factor
        row_max = jnp.max(scores, axis=-1, keepdims=True)
        exponent_terms = jnp.exp(scores - row_max)
        weights = (exponent_terms / jnp.sum(exponent_terms, axis=-1, keepdims=True)).astype(jnp.bfloat16)
        return jnp.einsum("ghqk,ghkd->ghqd", weights.astype(jnp.float32), value_rows.astype(jnp.float32)).astype(jnp.bfloat16)

    result = lax.map(attend_block, pieces)
    return jnp.moveaxis(result, 0, 2).reshape(queries.shape)


def heads_layer(operands):
    def per_head_attend(items):
        return attend_blocks(items[0][:, None], items[1][:, None], items[2][:, None])[:, 0]

    return lax.map(per_head_attend, operands)


def skip_heads(operands):
    return jnp.zeros_like(operands[0])


def reference(patch_qkv, kv_cache, text_kv, entering, gates, block_split, patch_index):
    new_cache = []
    attended = []
    leaving = []
    zero_index = jnp.zeros((), jnp.int32)
    for section_at in range(N_SECTION):
        gated_total = jnp.zeros((GUIDE, HEADS, PTOK * HD), jnp.float32)
        for inner_at in range(LAYERS):
            layer_at = section_at * LAYERS + inner_at
            fresh_rows = patch_qkv[layer_at].reshape(GUIDE, HEADS, 3, PTOK, HD)
            cached = kv_cache[layer_at].reshape(GUIDE, HEADS, 2, IMG, HD)
            slot_start = (patch_index[section_at] * PTOK).astype(jnp.int32)
            inserted = lax.dynamic_update_slice(cached, fresh_rows[:, :, 1:3], (zero_index, zero_index, zero_index, slot_start, zero_index))
            is_active = inner_at < block_split[section_at]
            new_cache.append(jnp.where(is_active, inserted, cached).reshape(kv_cache.shape[1:]))
            text_rows = text_kv[layer_at].reshape(GUIDE, HEADS, 2, TXT, HD)
            key_rows = jnp.concatenate([inserted[:, :, 0], text_rows[:, :, 0]], axis=2)
            value_rows = jnp.concatenate([inserted[:, :, 1], text_rows[:, :, 1]], axis=2)
            operands = (jnp.swapaxes(fresh_rows[:, :, 0], 0, 1), jnp.swapaxes(key_rows, 0, 1), jnp.swapaxes(value_rows, 0, 1))
            output_heads = jnp.swapaxes(lax.cond(is_active, heads_layer, skip_heads, operands), 0, 1)
            flat_out = output_heads.reshape(GUIDE, HEADS, PTOK * HD)
            attended.append(flat_out)
            gated_total = gated_total + gates[layer_at][:, :, None] * flat_out.astype(jnp.float32)
        branch = lax.optimization_barrier(gated_total.astype(jnp.bfloat16))
        leaving.append((entering[section_at].astype(jnp.float32) + branch.astype(jnp.float32)).astype(jnp.bfloat16))
    handed = jnp.roll(jnp.stack(leaving), 1, axis=0)
    return (jnp.stack(new_cache), jnp.stack(attended), handed)
```

```python
import math

import jax
import jax.numpy as jnp
from jax import lax
from jax.experimental import pallas as pl
from jax.experimental.pallas import tpu as pltpu
from jax.sharding import PartitionSpec as P

HD = 64
PATCHES = 4
TXT = 333
SEQ = 32
PAIRS = 128
ROWS = 512
STALE = 384
TROWS = 176
LG = 4
MESH = pl.DeviceIdType.MESH
BF = jnp.bfloat16
F32 = jnp.float32
FACTOR = HD ** (-0.5) * math.log2(math.e)


def low_rows(shape):
    return lax.broadcasted_iota(jnp.int32, shape, len(shape) - 2) < 4


def low_lanes(shape):
    return lax.broadcasted_iota(jnp.int32, shape, len(shape) - 1) < HD


def split_pieces(x):
    pieces = x.astype(F32).reshape(16, 2, 2, 8, 128)
    even, odd = pieces[:, 0], pieces[:, 1]
    even, odd = even.reshape(32, 8, 128), odd.reshape(32, 8, 128)
    mask = low_rows(even.shape)
    first = jnp.where(mask, even, pltpu.roll(odd, 4, 1)).reshape(16, 2, 8, 128)
    second = jnp.where(mask, pltpu.roll(even, 4, 1), odd).reshape(16, 2, 8, 128)
    return [
        half[:, layer].reshape(PAIRS, 128) for layer in range(2) for half in (first, second)
    ]


def kernel(
    patch_ref, split_ref, gates_ref, qkv_hbm, kv_hbm, text_hbm, ent_hbm,
    cache_hbm, att_hbm, hand_hbm,
    qkv_v, kv_v, text_v, ent_v, stage, tstage, send_q, send_kv, recv_q, recv_kv,
    keys, values, queries, maxima, partial,
    att_v, send_b, recv_b, hand_v,
    load_sem, q_send, q_recv, kv_send, kv_recv, e_send, e_recv, b_send, b_recv, out_sem,
):
    sections = lax.axis_size("section")
    sec = lax.axis_index("section")
    me = lax.axis_index("seq")
    after = lax.rem(sec + 1, sections)
    before = lax.rem(sec + sections - 1, sections)

    load_qkv = pltpu.make_async_copy(qkv_hbm, qkv_v, load_sem.at[0])
    load_kv = pltpu.make_async_copy(kv_hbm, kv_v, load_sem.at[1])
    load_text = pltpu.make_async_copy(text_hbm, text_v, load_sem.at[2])
    load_qkv.start()
    load_kv.start()
    load_text.start()

    barrier = pltpu.get_barrier_semaphore()

    def greet(step, carry):
        other = lax.rem(me + step, SEQ)
        pl.semaphore_signal(barrier, inc=1, device_id=(sec, other), device_id_type=MESH)
        return carry

    def greet_before(step, carry):
        other = lax.rem(me + step, SEQ)
        pl.semaphore_signal(barrier, inc=1, device_id=(before, other), device_id_type=MESH)
        return carry

    lax.fori_loop(1, SEQ, greet, 0)
    lax.fori_loop(0, SEQ, greet_before, 0)

    def arrange(part):
        for lg in range(LG):
            rows = qkv_v[lg * 3 + part].astype(F32)
            for at in range(4):
                stage[pl.ds(lg * 4 + at, SEQ, stride=16), :] = rows[:, at * 128:(at + 1) * 128]
        return stage[...].reshape(SEQ, 16, 128).astype(BF)

    load_qkv.wait()
    send_q[...] = arrange(0)
    pl.semaphore_wait(barrier, 2 * SEQ - 1)

    def q_copy(other):
        return pltpu.make_async_remote_copy(
            src_ref=send_q.at[other], dst_ref=recv_q.at[me], send_sem=q_send, recv_sem=q_recv,
            device_id=(sec, other), device_id_type=MESH,
        )

    def kv_copy(other):
        return pltpu.make_async_remote_copy(
            src_ref=send_kv.at[other], dst_ref=recv_kv.at[me], send_sem=kv_send, recv_sem=kv_recv,
            device_id=(sec, other), device_id_type=MESH,
        )

    def b_copy(other):
        return pltpu.make_async_remote_copy(
            src_ref=send_b.at[other], dst_ref=recv_b.at[me], send_sem=b_send, recv_sem=b_recv,
            device_id=(after, other), device_id_type=MESH,
        )

    def send_queries(step, carry):
        q_copy(lax.rem(me + step, SEQ)).start()
        return carry

    def send_pairs(step, carry):
        kv_copy(lax.rem(me + step, SEQ)).start()
        return carry

    def send_branch(step, carry):
        b_copy(lax.rem(me + step, SEQ)).start()
        return carry

    lax.fori_loop(1, SEQ, send_queries, 0)
    pltpu.make_async_copy(send_q.at[me], recv_q.at[me], q_recv).start()
    send_kv[:, :, 0:128] = arrange(1)
    send_kv[:, :, 128:256] = arrange(2)
    lax.fori_loop(1, SEQ, send_pairs, 0)
    pltpu.make_async_copy(send_kv.at[me], recv_kv.at[me], kv_recv).start()
    ent_copy = pltpu.make_async_remote_copy(
        src_ref=ent_hbm, dst_ref=ent_v, send_sem=e_send, recv_sem=e_recv,
        device_id=(after, me), device_id_type=MESH,
    )
    ent_copy.start()

    load_kv.wait()
    load_text.wait()

    slots = jnp.full((PAIRS, 128), patch_ref[0], jnp.int32)
    counts = jnp.full((PAIRS, 128), split_ref[0], jnp.int32)

    def prepare(lg, carry):
        tstage[...] = kv_v[lg].astype(F32)
        for at in range(PATCHES - 1):
            ahead = at < slots
            rows = pl.ds(at * PAIRS, PAIRS)
            here, later = at * 256, (at + 1) * 256
            keys[lg, rows, :] = jnp.where(
                ahead,
                tstage[pl.ds(here, PAIRS, stride=2), :],
                tstage[pl.ds(later, PAIRS, stride=2), :],
            ).astype(BF)
            values[lg, rows, 0:128] = jnp.where(
                ahead,
                tstage[pl.ds(here + 1, PAIRS, stride=2), :],
                tstage[pl.ds(later + 1, PAIRS, stride=2), :],
            ).astype(BF)
        values[lg, 0:STALE, 128:256] = jnp.ones((STALE, 128), BF)
        for at in range(TXT // 2):
            tstage[2 * at:2 * at + 2, :] = text_v[lg, :, at * 128:(at + 1) * 128].astype(F32)
        last = text_v[lg, :, TXT // 2 * 128:TXT * HD].astype(F32)
        last = jnp.concatenate([last, last], axis=1)
        row = lax.broadcasted_iota(jnp.int32, (TROWS, 128), 0)
        lane = lax.broadcasted_iota(jnp.int32, (TROWS, 128), 1)
        whole = row < TXT // 2
        half = (row == TXT // 2) & (lane < HD)
        keys[lg, STALE:, :] = jnp.where(whole, tstage[pl.ds(0, TROWS, stride=2), :], last[0:1]).astype(BF)
        end = jnp.where(half, last[1:2], 0.0)
        values[lg, STALE:, 0:128] = jnp.where(
            whole, tstage[pl.ds(1, TROWS, stride=2), :], end
        ).astype(BF)
        values[lg, STALE:, 128:256] = jnp.where(whole | half, 1.0, 0.0).astype(BF)
        return carry

    lax.fori_loop(0, LG, prepare, 0)

    pltpu.make_async_copy(recv_q, recv_q, q_recv).wait()
    lanes = low_lanes((PAIRS, 128))
    for lg, q in enumerate(split_pieces(recv_q[...])):
        turned = pltpu.roll(q, HD, 1)
        queries[lg, 0:128] = jnp.where(lanes, q, 0.0).astype(BF)
        queries[lg, 128:256] = jnp.where(lanes, turned, 0.0).astype(BF)
        queries[lg, 256:384] = jnp.where(lanes, 0.0, turned).astype(BF)
        queries[lg, 384:512] = jnp.where(lanes, 0.0, q).astype(BF)

    def scores_of(lg, k):
        return lax.dot_general(
            queries[lg], k, (((1,), (1,)), ((), ())), preferred_element_type=F32
        )

    def top(s):
        best = jnp.max(s, axis=1, keepdims=True)
        return jnp.maximum(best[0:256], best[256:512])

    def attend_stale(lg, carry):
        k = keys[lg]
        v = values[lg]
        s = scores_of(lg, k)
        best = top(s)
        maxima[lg] = jnp.broadcast_to(best, (256, 128))
        w = jnp.exp2((s - jnp.concatenate([best, best], axis=0)) * FACTOR).astype(BF)
        partial[lg] = jnp.dot(w, v, preferred_element_type=F32)
        return carry

    lax.fori_loop(0, LG, attend_stale, 0)

    pltpu.make_async_copy(recv_kv, recv_kv, kv_recv).wait()
    fresh_k = split_pieces(recv_kv[:, :, 0:128])
    fresh_v = split_pieces(recv_kv[:, :, 128:256])
    runs = [layer < counts for layer in range(2)]
    branch = [None, None]
    for lg in range(LG):
        layer, half = lg // 2, lg % 2
        tstage[pl.ds(0, PAIRS, stride=2), :] = fresh_k[lg]
        tstage[pl.ds(1, PAIRS, stride=2), :] = fresh_v[lg]
        for at in range(PATCHES * 2):
            here = runs[layer] & (slots == at // 2)
            rows = pl.ds(at * 128, 128)
            kv_v[lg, rows, :] = jnp.where(
                here, tstage[at % 2 * 128:(at % 2 + 1) * 128, :], kv_v[lg, rows, :].astype(F32)
            ).astype(BF)
        pltpu.make_async_copy(kv_v.at[lg], cache_hbm.at[lg], out_sem.at[0]).start()
    for lg in range(LG):
        layer, half = lg // 2, lg % 2
        s = scores_of(lg, fresh_k[lg].astype(BF))
        old = maxima[lg, :, 0:1]
        best = jnp.maximum(old, top(s))
        both = jnp.concatenate([best, best], axis=0)
        w = jnp.exp2((s - both) * FACTOR).astype(BF)
        v = jnp.concatenate([fresh_v[lg].astype(BF), jnp.ones((PAIRS, 128), BF)], axis=1)
        scale = jnp.exp2((old - best) * FACTOR)
        total = jnp.dot(w, v, preferred_element_type=F32)
        total = total + partial[lg] * jnp.concatenate([scale, scale], axis=0)

        def joined(part):
            a, b, c, d = (part[at * 128:(at + 1) * 128] for at in range(4))
            return jnp.where(lanes, a + pltpu.roll(c, HD, 1), pltpu.roll(b, HD, 1) + d)

        out = joined(total[:, 0:128]) / joined(total[:, 128:256])
        out = jnp.where(runs[layer], out, 0.0).astype(BF).astype(F32)
        stage[pl.ds(layer * 256 + half, PAIRS, stride=2), :] = out
        gated = gates_ref[layer, half, me] * out
        branch[half] = gated if branch[half] is None else branch[half] + gated

    first, second = (part.reshape(16, 8, 128) for part in branch)
    mask = low_rows(first.shape)
    even = jnp.where(mask, first, pltpu.roll(second, 4, 1))
    odd = jnp.where(mask, pltpu.roll(first, 4, 1), second)
    send_b[...] = jnp.stack([even, odd], axis=1).reshape(SEQ, 8, 128).astype(BF)
    lax.fori_loop(0, SEQ, send_branch, 0)
    att_v[...] = stage[...].astype(BF)
    store_att = pltpu.make_async_copy(att_v, att_hbm, out_sem.at[1])
    store_att.start()

    ent_copy.wait()
    pltpu.make_async_copy(recv_b, recv_b, b_recv).wait()
    tstage[0:256, :] = recv_b[...].astype(F32).reshape(256, 128)
    for half in range(2):
        for at in range(4):
            cols = pl.ds(at * 128, 128)
            moved = tstage[pl.ds(half * 4 + at, SEQ, stride=8), :]
            hand_v[half, :, cols] = (ent_v[half, :, cols].astype(F32) + moved).astype(BF)
    store_hand = pltpu.make_async_copy(hand_v, hand_hbm, out_sem.at[2])
    store_hand.start()

    pltpu.make_async_copy(send_b, send_b, b_send).wait()
    rest = pl.ds(0, SEQ - 1)
    pltpu.make_async_copy(send_q.at[rest], send_q.at[rest], q_send).wait()
    pltpu.make_async_copy(send_kv.at[rest], send_kv.at[rest], kv_send).wait()
    pltpu.make_async_copy(kv_v, cache_hbm, out_sem.at[0]).wait()
    store_att.wait()
    store_hand.wait()


def on_device(patch_qkv, kv_cache, text_kv, entering, gates, block_split, patch_index):
    qkv = jnp.transpose(patch_qkv, (0, 1, 3, 2, 4)).reshape(12, SEQ, 512)
    kv = kv_cache.reshape(LG, 2, ROWS, 128).transpose(0, 2, 1, 3).reshape(LG, 2 * ROWS, 128)
    text = text_kv.reshape(LG, 2, TXT * HD)
    ent = entering.reshape(2, SEQ, 512)
    hbm = pl.BlockSpec(memory_space=pl.ANY)
    smem = pl.BlockSpec(memory_space=pltpu.SMEM)
    vmem = pltpu.VMEM
    cache, att, handed = pl.pallas_call(
        kernel,
        out_shape=[
            jax.ShapeDtypeStruct((LG, 2 * ROWS, 128), BF),
            jax.ShapeDtypeStruct((4 * PAIRS, 128), BF),
            jax.ShapeDtypeStruct((2, SEQ, 512), BF),
        ],
        in_specs=[smem, smem, smem, hbm, hbm, hbm, hbm],
        out_specs=[hbm, hbm, hbm],
        scratch_shapes=[
            vmem((12, SEQ, 512), BF),
            vmem((LG, 2 * ROWS, 128), BF),
            vmem((LG, 2, TXT * HD), BF),
            vmem((2, SEQ, 512), BF),
            vmem((ROWS, 128), F32),
            vmem((2 * ROWS, 128), F32),
            vmem((SEQ, 16, 128), BF),
            vmem((SEQ, 16, 256), BF),
            vmem((SEQ, 16, 128), BF),
            vmem((SEQ, 16, 256), BF),
            vmem((LG, STALE + TROWS, 128), BF),
            vmem((LG, STALE + TROWS, 256), BF),
            vmem((LG, 4 * PAIRS, 128), BF),
            vmem((LG, 2 * PAIRS, 128), F32),
            vmem((LG, 4 * PAIRS, 256), F32),
            vmem((4 * PAIRS, 128), BF),
            vmem((SEQ, 8, 128), BF),
            vmem((SEQ, 8, 128), BF),
            vmem((2, SEQ, 512), BF),
            pltpu.SemaphoreType.DMA((3,)),
            pltpu.SemaphoreType.DMA,
            pltpu.SemaphoreType.DMA,
            pltpu.SemaphoreType.DMA,
            pltpu.SemaphoreType.DMA,
            pltpu.SemaphoreType.DMA,
            pltpu.SemaphoreType.DMA,
            pltpu.SemaphoreType.DMA,
            pltpu.SemaphoreType.DMA,
            pltpu.SemaphoreType.DMA((3,)),
        ],
        compiler_params=pltpu.CompilerParams(
            collective_id=0, has_side_effects=True, vmem_limit_bytes=56 * 1024 * 1024
        ),
    )(patch_index, block_split, gates, qkv, kv, text, ent)
    cache = cache.reshape(LG, ROWS, 2, 128).transpose(0, 2, 1, 3).reshape(kv_cache.shape)
    att = att.reshape(2, PAIRS, 2, 128).transpose(0, 2, 1, 3).reshape(2, 2, 1, 2 * PAIRS * HD)
    return cache, att, handed.reshape(entering.shape)


def solution(mesh):
    in_specs = (
        P("section", None, None, None, "seq"),
        P("section", None, "seq", None, None),
        P("section", None, "seq", None, None),
        P("section", None, None, "seq"),
        P("section", None, None),
        P("section"),
        P("section"),
    )
    out_specs = (
        P("section", None, "seq", None, None),
        P("section", None, "seq", None),
        P("section", None, None, "seq"),
    )
    return jax.shard_map(
        on_device, mesh=mesh, in_specs=in_specs, out_specs=out_specs, check_vma=False
    )
```

```python
import math

import jax
import jax.numpy as jnp
from jax import lax
from jax.experimental import pallas as pl
from jax.experimental.pallas import tpu as pltpu
from jax.sharding import PartitionSpec as P

HD = 64
PATCHES = 4
TXT = 333
SEQ = 32
PAIRS = 128
ROWS = 512
STALE = 384
TROWS = 176
NKEY = STALE + TROWS
VROWS = 144
LG = 4
MESH = pl.DeviceIdType.MESH
BF = jnp.bfloat16
F32 = jnp.float32
FACTOR = HD ** (-0.5) * math.log2(math.e)


def far_first():
    hops = (0, 1, 2, 1)
    return sorted(range(1, SEQ), key=lambda flip: -(hops[flip // 8] + hops[flip // 2 % 4]))


def low_rows(shape):
    return lax.broadcasted_iota(jnp.int32, shape, len(shape) - 2) < 4


def split_pieces(x):
    pieces = x.astype(F32).reshape(16, 2, 2, 8, 128)
    even, odd = pieces[:, 0], pieces[:, 1]
    even, odd = even.reshape(32, 8, 128), odd.reshape(32, 8, 128)
    mask = low_rows(even.shape)
    first = jnp.where(mask, even, pltpu.roll(odd, 4, 1)).reshape(16, 2, 8, 128)
    second = jnp.where(mask, pltpu.roll(even, 4, 1), odd).reshape(16, 2, 8, 128)
    return [
        half[:, layer].reshape(PAIRS, 128) for layer in range(2) for half in (first, second)
    ]


def kernel(
    patch_s, split_s, gates_hbm, qkv_hbm, kv_hbm, text_hbm, ent_hbm,
    cache, att, hand,
    gates_v, qkv_v, text_v, ent_v, stage, tstage,
    send_q, send_kv, recv_q, recv_kv, keys, values, queries, send_b, recv_b,
    load_sem, q_send, q_recv, kv_send, kv_recv, e_send, e_recv, b_send, b_recv, ready_sem,
):
    sections = lax.axis_size("section")
    sec = lax.axis_index("section")
    me = lax.axis_index("seq")
    after = lax.rem(sec + 1, sections)
    before = lax.rem(sec + sections - 1, sections)

    load_qkv = pltpu.make_async_copy(qkv_hbm, qkv_v, load_sem.at[0])
    load_kv = pltpu.make_async_copy(kv_hbm, cache, load_sem.at[1])
    load_text = pltpu.make_async_copy(text_hbm, text_v, load_sem.at[2])
    load_gates = pltpu.make_async_copy(gates_hbm, gates_v, load_sem.at[3])
    load_qkv.start()

    barrier = pltpu.get_barrier_semaphore()
    for other in (after, before):
        pl.semaphore_signal(barrier, inc=1, device_id=(other, me), device_id_type=MESH)
    for flip in far_first():
        pl.semaphore_signal(
            barrier, inc=1, device_id=(sec, jnp.bitwise_xor(me, flip)), device_id_type=MESH
        )
    load_kv.start()
    load_text.start()
    load_gates.start()

    def arrange(part):
        for lg in range(LG):
            rows = qkv_v[lg * 3 + part].astype(F32)
            for at in range(4):
                stage[pl.ds(lg * 4 + at, SEQ, stride=16), :] = rows[:, at * 128:(at + 1) * 128]
        return stage[...].reshape(SEQ, 16, 128).astype(BF)

    load_qkv.wait()
    send_q[...] = arrange(0)
    pl.semaphore_wait(barrier, SEQ + 1)

    def q_copy(other):
        return pltpu.make_async_remote_copy(
            src_ref=send_q.at[other], dst_ref=recv_q.at[me], send_sem=q_send, recv_sem=q_recv,
            device_id=(sec, other), device_id_type=MESH,
        )

    def kv_copy(other):
        return pltpu.make_async_remote_copy(
            src_ref=send_kv.at[other], dst_ref=recv_kv.at[me], send_sem=kv_send, recv_sem=kv_recv,
            device_id=(sec, other), device_id_type=MESH,
        )

    def b_copy(other):
        return pltpu.make_async_remote_copy(
            src_ref=send_b.at[other], dst_ref=recv_b.at[me], send_sem=b_send, recv_sem=b_recv,
            device_id=(after, other), device_id_type=MESH,
        )

    for flip in far_first():
        q_copy(jnp.bitwise_xor(me, flip)).start()
    pltpu.make_async_copy(send_q.at[me], recv_q.at[me], q_recv).start()
    send_kv[:, :, 0:128] = arrange(1)
    send_kv[:, :, 128:256] = arrange(2)
    for flip in far_first():
        kv_copy(jnp.bitwise_xor(me, flip)).start()
    pltpu.make_async_copy(send_kv.at[me], recv_kv.at[me], kv_recv).start()
    pl.semaphore_signal(ready_sem, inc=1, device_id=(before, me), device_id_type=MESH)
    ent_copy = pltpu.make_async_remote_copy(
        src_ref=ent_hbm, dst_ref=ent_v, send_sem=e_send, recv_sem=e_recv,
        device_id=(after, me), device_id_type=MESH,
    )
    ent_copy.start()

    load_kv.wait()
    load_text.wait()
    load_gates.wait()
    slots = jnp.full((PAIRS, 128), patch_s[0], jnp.int32)
    counts = jnp.full((PAIRS, 128), split_s[0], jnp.int32)
    column = lax.broadcasted_iota(jnp.int32, (VROWS - 128, NKEY), 1)
    evens = lax.broadcasted_iota(jnp.int32, (VROWS - 128, NKEY), 0) < 8
    whole_pairs = STALE + TXT // 2
    counted = (column < whole_pairs) | ((column == whole_pairs) & evens)
    ones = jnp.where(counted, 1.0, 0.0).astype(BF)

    def prepare(lg, carry):
        tstage[...] = cache[lg].astype(F32)
        for at in range(PATCHES - 1):
            ahead = at < slots
            rows = pl.ds(at * PAIRS, PAIRS)
            here, later = at * 256, (at + 1) * 256
            keys[lg, rows, :] = jnp.where(
                ahead,
                tstage[pl.ds(here, PAIRS, stride=2), :],
                tstage[pl.ds(later, PAIRS, stride=2), :],
            ).astype(BF)
            values[lg, 0:128, rows] = jnp.where(
                ahead,
                tstage[pl.ds(here + 1, PAIRS, stride=2), :],
                tstage[pl.ds(later + 1, PAIRS, stride=2), :],
            ).T.astype(BF)
        for at in range(TXT // 2):
            tstage[2 * at:2 * at + 2, :] = text_v[lg, :, at * 128:(at + 1) * 128].astype(F32)
        last = text_v[lg, :, TXT // 2 * 128:TXT * HD].astype(F32)
        last = jnp.concatenate([last, last], axis=1)
        row = lax.broadcasted_iota(jnp.int32, (TROWS, 128), 0)
        lane = lax.broadcasted_iota(jnp.int32, (TROWS, 128), 1)
        whole = row < TXT // 2
        half = (row == TXT // 2) & (lane < HD)
        keys[lg, STALE:, :] = jnp.where(
            whole, tstage[pl.ds(0, TROWS, stride=2), :], last[0:1]
        ).astype(BF)
        end = jnp.where(half, last[1:2], 0.0)
        values[lg, 0:128, STALE:] = jnp.where(
            whole, tstage[pl.ds(1, TROWS, stride=2), :], end
        ).T.astype(BF)
        values[lg, 128:, :] = ones
        return carry

    lax.fori_loop(0, LG, prepare, 0)

    pltpu.make_async_copy(recv_q, recv_q, q_recv).wait()
    lanes = lax.broadcasted_iota(jnp.int32, (PAIRS, 128), 1) < HD
    for lg, q in enumerate(split_pieces(recv_q[...])):
        turned = pltpu.roll(q, HD, 1)
        queries[lg, 0:128] = jnp.where(lanes, q, 0.0).astype(BF)
        queries[lg, 128:256] = jnp.where(lanes, turned, 0.0).astype(BF)
        queries[lg, 256:384] = jnp.where(lanes, 0.0, turned).astype(BF)
        queries[lg, 384:512] = jnp.where(lanes, 0.0, q).astype(BF)

    def scores_of(lg, k):
        s = lax.dot_general(k, queries[lg], (((1,), (1,)), ((), ())), preferred_element_type=F32)
        best = jnp.max(s, axis=0, keepdims=True)
        return s, jnp.maximum(best[:, 0:256], best[:, 256:512])

    def twice(x):
        return jnp.concatenate([x, x], axis=1)

    old, partial = [], []
    for lg in range(LG):
        s, best = scores_of(lg, keys[lg])
        w = jnp.exp2((s - twice(best)) * FACTOR).astype(BF)
        old.append(best)
        partial.append(jnp.dot(values[lg], w, preferred_element_type=F32))

    pltpu.make_async_copy(recv_kv, recv_kv, kv_recv).wait()
    fresh_k = split_pieces(recv_kv[:, :, 0:128])
    fresh_v = split_pieces(recv_kv[:, :, 128:256])
    attended, branch = [], [None, None]
    mine = lax.broadcasted_iota(jnp.int32, (2, SEQ), 1) == me
    for lg in range(LG):
        layer, half = lg // 2, lg % 2
        s, best = scores_of(lg, fresh_k[lg].astype(BF))
        best = jnp.maximum(old[lg], best)
        w = jnp.exp2((s - twice(best)) * FACTOR).astype(BF)
        v = jnp.concatenate(
            [fresh_v[lg].T.astype(BF), jnp.ones((VROWS - 128, PAIRS), BF)], axis=0
        )
        scale = jnp.exp2((old[lg] - best) * FACTOR)
        total = jnp.dot(v, w, preferred_element_type=F32) + partial[lg] * twice(scale)

        def joined(at, low, high, size):
            cols = slice(at * 128, at * 128 + 128)
            cols2 = slice(at * 128 + 256, at * 128 + 384)
            return total[low:low + size, cols] + total[high:high + size, cols2]

        out = jnp.concatenate(
            [joined(at, 0, 64, 64) / joined(at, 128, 136, 8)[0:1] for at in range(2)], axis=0
        ).T
        out = jnp.where(layer < counts, out, 0.0).astype(BF).astype(F32)
        attended.append(out)
        gate = jnp.sum(jnp.where(mine, gates_v[layer], 0.0), axis=1, keepdims=True)
        gated = gate[half:half + 1] * out
        branch[half] = gated if branch[half] is None else branch[half] + gated

    first, second = (part.reshape(16, 8, 128) for part in branch)
    mask = low_rows(first.shape)
    even = jnp.where(mask, first, pltpu.roll(second, 4, 1))
    odd = jnp.where(mask, pltpu.roll(first, 4, 1), second)
    send_b[...] = jnp.stack([even, odd], axis=1).reshape(SEQ, 8, 128).astype(BF)
    pl.semaphore_wait(ready_sem, 1)
    for flip in far_first() + [0]:
        b_copy(jnp.bitwise_xor(me, flip)).start()

    for lg in range(LG):
        layer, half = lg // 2, lg % 2
        tstage[pl.ds(lg * 256, PAIRS, stride=2), :] = fresh_k[lg]
        tstage[pl.ds(lg * 256 + 1, PAIRS, stride=2), :] = fresh_v[lg]
        for at in range(PATCHES * 2):
            here = (layer < counts) & (slots == at // 2)
            rows = pl.ds(at * 128, 128)
            fresh = tstage[pl.ds(lg * 256 + at % 2 * 128, 128), :]
            cache[lg, rows, :] = jnp.where(here, fresh, cache[lg, rows, :].astype(F32)).astype(BF)
        stage[pl.ds(layer * 256 + half, PAIRS, stride=2), :] = attended[lg]
    att[...] = stage[...].astype(BF)

    ent_copy.wait()
    pltpu.make_async_copy(recv_b, recv_b, b_recv).wait()
    tstage[0:256, :] = recv_b[...].astype(F32).reshape(256, 128)
    for half in range(2):
        for at in range(4):
            cols = pl.ds(at * 128, 128)
            moved = tstage[pl.ds(half * 4 + at, SEQ, stride=8), :]
            hand[half, :, cols] = (ent_v[half, :, cols].astype(F32) + moved).astype(BF)

    pltpu.make_async_copy(send_b, send_b, b_send).wait()
    rest = pl.ds(0, SEQ - 1)
    pltpu.make_async_copy(send_q.at[rest], send_q.at[rest], q_send).wait()
    pltpu.make_async_copy(send_kv.at[rest], send_kv.at[rest], kv_send).wait()


def on_device(patch_qkv, kv_cache, text_kv, entering, gates, block_split, patch_index):
    qkv = jnp.transpose(patch_qkv, (0, 1, 3, 2, 4)).reshape(12, SEQ, 512)
    kv = kv_cache.reshape(LG, 2, ROWS, 128).transpose(0, 2, 1, 3).reshape(LG, 2 * ROWS, 128)
    text = text_kv.reshape(LG, 2, TXT * HD)
    ent = entering.reshape(2, SEQ, 512)
    large = [
        pltpu.with_memory_space_constraint(operand, pltpu.HBM)
        for operand in (gates, qkv, kv, text, ent)
    ]
    vmem = pltpu.VMEM
    cache, att, handed = pl.pallas_call(
        kernel,
        out_shape=[
            vmem((LG, 2 * ROWS, 128), BF),
            vmem((4 * PAIRS, 128), BF),
            vmem((2, SEQ, 512), BF),
        ],
        in_specs=[pl.BlockSpec(memory_space=pltpu.SMEM)] * 2
        + [pl.BlockSpec(memory_space=pltpu.HBM)] * 5,
        out_specs=[pl.BlockSpec(memory_space=vmem)] * 3,
        scratch_shapes=[
            vmem((2, 2, SEQ), F32),
            vmem((12, SEQ, 512), BF),
            vmem((LG, 2, TXT * HD), BF),
            vmem((2, SEQ, 512), BF),
            vmem((ROWS, 128), F32),
            vmem((2 * ROWS, 128), F32),
            vmem((SEQ, 16, 128), BF),
            vmem((SEQ, 16, 256), BF),
            vmem((SEQ, 16, 128), BF),
            vmem((SEQ, 16, 256), BF),
            vmem((LG, NKEY, 128), BF),
            vmem((LG, VROWS, NKEY), BF),
            vmem((LG, 4 * PAIRS, 128), BF),
            vmem((SEQ, 8, 128), BF),
            vmem((SEQ, 8, 128), BF),
            pltpu.SemaphoreType.DMA((4,)),
            pltpu.SemaphoreType.DMA,
            pltpu.SemaphoreType.DMA,
            pltpu.SemaphoreType.DMA,
            pltpu.SemaphoreType.DMA,
            pltpu.SemaphoreType.DMA,
            pltpu.SemaphoreType.DMA,
            pltpu.SemaphoreType.DMA,
            pltpu.SemaphoreType.DMA,
            pltpu.SemaphoreType.REGULAR,
        ],
        compiler_params=pltpu.CompilerParams(
            collective_id=0, has_side_effects=True, vmem_limit_bytes=48 * 1024 * 1024
        ),
    )(patch_index, block_split, *large)
    cache = cache.reshape(LG, ROWS, 2, 128).transpose(0, 2, 1, 3).reshape(kv_cache.shape)
    att = att.reshape(2, PAIRS, 2, 128).transpose(0, 2, 1, 3).reshape(2, 2, 1, 2 * PAIRS * HD)
    return cache, att, handed.reshape(entering.shape)


def solution(mesh):
    in_specs = (
        P("section", None, None, None, "seq"),
        P("section", None, "seq", None, None),
        P("section", None, "seq", None, None),
        P("section", None, None, "seq"),
        P("section", None, None),
        P("section"),
        P("section"),
    )
    out_specs = (
        P("section", None, "seq", None, None),
        P("section", None, "seq", None),
        P("section", None, None, "seq"),
    )
    return jax.shard_map(
        on_device, mesh=mesh, in_specs=in_specs, out_specs=out_specs, check_vma=False
    )
```

```python
import math

import jax
import jax.numpy as jnp
from jax import lax
from jax.experimental import pallas as pl
from jax.experimental.pallas import tpu as pltpu
from jax.sharding import PartitionSpec as P

HD = 64
PATCHES = 4
TXT = 333
SEQ = 32
PAIRS = 128
ROWS = 512
STALE = 384
TROWS = 176
NKEY = STALE + TROWS
VROWS = 144
LG = 4
MESH = pl.DeviceIdType.MESH
BF = jnp.bfloat16
F32 = jnp.float32
FACTOR = HD ** (-0.5) * math.log2(math.e)


def far_first():
    hops = (0, 1, 2, 1)
    return sorted(range(1, SEQ), key=lambda flip: -(hops[flip // 8] + hops[flip // 2 % 4]))


def low_rows(shape):
    return lax.broadcasted_iota(jnp.int32, shape, len(shape) - 2) < 4


def split_pieces(x):
    pieces = x.astype(F32).reshape(16, 2, 2, 8, 128)
    even, odd = pieces[:, 0], pieces[:, 1]
    even, odd = even.reshape(32, 8, 128), odd.reshape(32, 8, 128)
    mask = low_rows(even.shape)
    first = jnp.where(mask, even, pltpu.roll(odd, 4, 1)).reshape(16, 2, 8, 128)
    second = jnp.where(mask, pltpu.roll(even, 4, 1), odd).reshape(16, 2, 8, 128)
    return [
        inner[:, outer].reshape(PAIRS, 128) for outer in range(2) for inner in (first, second)
    ]


def kernel(
    patch_s, split_s, gates_hbm, qkv_hbm, kv_hbm, text_hbm, ent_hbm,
    cache, att, recv_b, ent_v,
    gates_v, qkv_v, text_v, stage, tstage,
    send_q, send_kv, recv_q, recv_kv, keys, values, queries, send_b,
    load_sem, q_send, q_recv, kv_send, kv_recv, e_send, e_recv, b_send, b_recv, ready_sem,
):
    sections = lax.axis_size("section")
    sec = lax.axis_index("section")
    me = lax.axis_index("seq")
    after = lax.rem(sec + 1, sections)
    before = lax.rem(sec + sections - 1, sections)

    load_qkv = pltpu.make_async_copy(qkv_hbm, qkv_v, load_sem.at[0])
    load_kv = pltpu.make_async_copy(kv_hbm, cache, load_sem.at[1])
    load_text = pltpu.make_async_copy(text_hbm, text_v, load_sem.at[2])
    load_gates = pltpu.make_async_copy(gates_hbm, gates_v, load_sem.at[3])
    load_qkv.start()

    barrier = pltpu.get_barrier_semaphore()
    for other in (after, before):
        pl.semaphore_signal(barrier, inc=1, device_id=(other, me), device_id_type=MESH)
    for flip in far_first():
        pl.semaphore_signal(
            barrier, inc=1, device_id=(sec, jnp.bitwise_xor(me, flip)), device_id_type=MESH
        )
    load_kv.start()
    load_text.start()
    load_gates.start()

    def arrange(parts):
        for place, part in enumerate(parts):
            rows = qkv_v[part].astype(F32)
            for at in range(4):
                stage[pl.ds(place * 4 + at, SEQ, stride=16), :] = rows[:, at * 128:(at + 1) * 128]
        return stage[...].reshape(SEQ, 16, 128).astype(BF)

    load_qkv.wait()
    send_q[...] = arrange([0, 3, 6, 9])
    pl.semaphore_wait(barrier, SEQ + 1)

    def q_copy(other):
        return pltpu.make_async_remote_copy(
            src_ref=send_q.at[other], dst_ref=recv_q.at[me], send_sem=q_send, recv_sem=q_recv,
            device_id=(sec, other), device_id_type=MESH,
        )

    def kv_copy(half, other):
        return pltpu.make_async_remote_copy(
            src_ref=send_kv.at[half, other], dst_ref=recv_kv.at[half, me],
            send_sem=kv_send.at[half], recv_sem=kv_recv.at[half],
            device_id=(sec, other), device_id_type=MESH,
        )

    def b_copy(half, other):
        return pltpu.make_async_remote_copy(
            src_ref=send_b.at[half, other], dst_ref=recv_b.at[half, me],
            send_sem=b_send.at[half], recv_sem=b_recv.at[half],
            device_id=(after, other), device_id_type=MESH,
        )

    for flip in far_first():
        q_copy(jnp.bitwise_xor(me, flip)).start()
    pltpu.make_async_copy(send_q.at[me], recv_q.at[me], q_recv).start()
    for half in range(2):
        first = half * 3
        send_kv[half] = arrange([first + 1, first + 7, first + 2, first + 8])
        for flip in far_first():
            kv_copy(half, jnp.bitwise_xor(me, flip)).start()
        pltpu.make_async_copy(
            send_kv.at[half, me], recv_kv.at[half, me], kv_recv.at[half]
        ).start()
    pl.semaphore_signal(ready_sem, inc=1, device_id=(before, me), device_id_type=MESH)
    ent_copy = pltpu.make_async_remote_copy(
        src_ref=ent_hbm, dst_ref=ent_v, send_sem=e_send, recv_sem=e_recv,
        device_id=(after, me), device_id_type=MESH,
    )
    ent_copy.start()

    load_kv.wait()
    load_text.wait()
    load_gates.wait()
    slots = jnp.full((PAIRS, 128), patch_s[0], jnp.int32)
    counts = jnp.full((PAIRS, 128), split_s[0], jnp.int32)
    column = lax.broadcasted_iota(jnp.int32, (VROWS - 128, NKEY), 1)
    evens = lax.broadcasted_iota(jnp.int32, (VROWS - 128, NKEY), 0) < 8
    whole_pairs = STALE + TXT // 2
    counted = (column < whole_pairs) | ((column == whole_pairs) & evens)
    ones = jnp.where(counted, 1.0, 0.0).astype(BF)

    def prepare(lg, carry):
        tstage[...] = cache[lg].astype(F32)
        for at in range(PATCHES - 1):
            ahead = at < slots
            rows = pl.ds(at * PAIRS, PAIRS)
            here, later = at * 256, (at + 1) * 256
            keys[lg, rows, :] = jnp.where(
                ahead,
                tstage[pl.ds(here, PAIRS, stride=2), :],
                tstage[pl.ds(later, PAIRS, stride=2), :],
            ).astype(BF)
            values[lg, 0:128, rows] = jnp.where(
                ahead,
                tstage[pl.ds(here + 1, PAIRS, stride=2), :],
                tstage[pl.ds(later + 1, PAIRS, stride=2), :],
            ).T.astype(BF)
        for at in range(TXT // 2):
            tstage[2 * at:2 * at + 2, :] = text_v[lg, :, at * 128:(at + 1) * 128].astype(F32)
        last = text_v[lg, :, TXT // 2 * 128:TXT * HD].astype(F32)
        last = jnp.concatenate([last, last], axis=1)
        row = lax.broadcasted_iota(jnp.int32, (TROWS, 128), 0)
        lane = lax.broadcasted_iota(jnp.int32, (TROWS, 128), 1)
        whole = row < TXT // 2
        half = (row == TXT // 2) & (lane < HD)
        keys[lg, STALE:, :] = jnp.where(
            whole, tstage[pl.ds(0, TROWS, stride=2), :], last[0:1]
        ).astype(BF)
        end = jnp.where(half, last[1:2], 0.0)
        values[lg, 0:128, STALE:] = jnp.where(
            whole, tstage[pl.ds(1, TROWS, stride=2), :], end
        ).T.astype(BF)
        values[lg, 128:, :] = ones
        return carry

    lax.fori_loop(0, LG, prepare, 0)

    pltpu.make_async_copy(recv_q, recv_q, q_recv).wait()
    lanes = lax.broadcasted_iota(jnp.int32, (PAIRS, 128), 1) < HD
    for lg, q in enumerate(split_pieces(recv_q[...])):
        turned = pltpu.roll(q, HD, 1)
        queries[lg, 0:128] = jnp.where(lanes, q, 0.0).astype(BF)
        queries[lg, 128:256] = jnp.where(lanes, turned, 0.0).astype(BF)
        queries[lg, 256:384] = jnp.where(lanes, 0.0, turned).astype(BF)
        queries[lg, 384:512] = jnp.where(lanes, 0.0, q).astype(BF)

    def scores_of(lg, k):
        s = lax.dot_general(k, queries[lg], (((1,), (1,)), ((), ())), preferred_element_type=F32)
        best = jnp.max(s, axis=0, keepdims=True)
        return s, jnp.maximum(best[:, 0:256], best[:, 256:512])

    def twice(x):
        return jnp.concatenate([x, x], axis=1)

    old, partial = [None] * LG, [None] * LG
    for lg in (0, 2, 1, 3):
        s, best = scores_of(lg, keys[lg])
        w = jnp.exp2((s - twice(best)) * FACTOR).astype(BF)
        old[lg] = best
        partial[lg] = jnp.dot(values[lg], w, preferred_element_type=F32)

    mine = lax.broadcasted_iota(jnp.int32, (2, SEQ), 1) == me
    gate = [
        jnp.sum(jnp.where(mine, gates_v[layer], 0.0), axis=1, keepdims=True) for layer in range(2)
    ]

    def attend_fresh(lg, k, v):
        s, best = scores_of(lg, k.astype(BF))
        best = jnp.maximum(old[lg], best)
        w = jnp.exp2((s - twice(best)) * FACTOR).astype(BF)
        v = jnp.concatenate([v.T.astype(BF), jnp.ones((VROWS - 128, PAIRS), BF)], axis=0)
        scale = jnp.exp2((old[lg] - best) * FACTOR)
        total = jnp.dot(v, w, preferred_element_type=F32) + partial[lg] * twice(scale)

        def joined(at, low, high, size):
            cols = slice(at * 128, at * 128 + 128)
            cols2 = slice(at * 128 + 256, at * 128 + 384)
            return total[low:low + size, cols] + total[high:high + size, cols2]

        out = jnp.concatenate(
            [joined(at, 0, 64, 64) / joined(at, 128, 136, 8)[0:1] for at in range(2)], axis=0
        ).T
        return jnp.where(lg // 2 < counts, out, 0.0).astype(BF).astype(F32)

    fresh, attended = [None] * LG, [None] * LG
    for half in range(2):
        pltpu.make_async_copy(recv_kv.at[half], recv_kv.at[half], kv_recv.at[half]).wait()
        pieces = split_pieces(recv_kv[half])
        branch = None
        for layer in range(2):
            lg = layer * 2 + half
            fresh[lg] = pieces[layer], pieces[2 + layer]
            attended[lg] = attend_fresh(lg, *fresh[lg])
            gated = gate[layer][half:half + 1] * attended[lg]
            branch = gated if branch is None else branch + gated
        send_b[half] = branch.reshape(SEQ, 4, 128).astype(BF)
        if half == 0:
            pl.semaphore_wait(ready_sem, 1)
        for flip in far_first() + [0]:
            b_copy(half, jnp.bitwise_xor(me, flip)).start()

    for lg in range(LG):
        layer, half = lg // 2, lg % 2
        tstage[pl.ds(lg * 256, PAIRS, stride=2), :] = fresh[lg][0]
        tstage[pl.ds(lg * 256 + 1, PAIRS, stride=2), :] = fresh[lg][1]
        for at in range(PATCHES * 2):
            here = (layer < counts) & (slots == at // 2)
            rows = pl.ds(at * 128, 128)
            new = tstage[pl.ds(lg * 256 + at % 2 * 128, 128), :]
            cache[lg, rows, :] = jnp.where(here, new, cache[lg, rows, :].astype(F32)).astype(BF)
        stage[pl.ds(layer * 256 + half, PAIRS, stride=2), :] = attended[lg]
    att[...] = stage[...].astype(BF)

    rest = pl.ds(0, SEQ - 1)
    pltpu.make_async_copy(send_q.at[rest], send_q.at[rest], q_send).wait()
    for half in range(2):
        part = send_kv.at[half, rest]
        pltpu.make_async_copy(part, part, kv_send.at[half]).wait()
    ent_copy.wait()
    for half in range(2):
        pltpu.make_async_copy(send_b.at[half], send_b.at[half], b_send.at[half]).wait()
        pltpu.make_async_copy(recv_b.at[half], recv_b.at[half], b_recv.at[half]).wait()


def write_out(
    cache, att, recv_b, ent_v, cache_hbm, att_hbm, hand_hbm, moved, hand, sem
):
    copies = [pltpu.make_async_copy(cache.at[lg], cache_hbm.at[lg], sem.at[lg]) for lg in range(LG)]
    copies.append(pltpu.make_async_copy(att, att_hbm, sem.at[4]))
    for copy in copies:
        copy.start()
    for half in range(2):
        moved[...] = recv_b[half].astype(F32).reshape(PAIRS, 128)
        for at in range(4):
            cols = pl.ds(at * 128, 128)
            branch = moved[pl.ds(at, SEQ, stride=4), :]
            hand[half, :, cols] = (ent_v[half, :, cols].astype(F32) + branch).astype(BF)
    copies.append(pltpu.make_async_copy(hand, hand_hbm, sem.at[5]))
    copies[-1].start()
    for copy in copies:
        copy.wait()


def on_device(patch_qkv, kv_cache, text_kv, entering, gates, block_split, patch_index):
    qkv = jnp.transpose(patch_qkv, (0, 1, 3, 2, 4)).reshape(12, SEQ, 512)
    kv = kv_cache.reshape(LG, 2, ROWS, 128).transpose(0, 2, 1, 3).reshape(LG, 2 * ROWS, 128)
    text = text_kv.reshape(LG, 2, TXT * HD)
    ent = entering.reshape(2, SEQ, 512)
    large = [
        pltpu.with_memory_space_constraint(operand, pltpu.HBM)
        for operand in (gates, qkv, kv, text, ent)
    ]
    vmem = pltpu.VMEM
    kept = pl.pallas_call(
        kernel,
        out_shape=[
            vmem((LG, 2 * ROWS, 128), BF),
            vmem((4 * PAIRS, 128), BF),
            vmem((2, SEQ, 4, 128), BF),
            vmem((2, SEQ, 512), BF),
        ],
        in_specs=[pl.BlockSpec(memory_space=pltpu.SMEM)] * 2
        + [pl.BlockSpec(memory_space=pltpu.HBM)] * 5,
        out_specs=[pl.BlockSpec(memory_space=vmem)] * 4,
        scratch_shapes=[
            vmem((2, 2, SEQ), F32),
            vmem((12, SEQ, 512), BF),
            vmem((LG, 2, TXT * HD), BF),
            vmem((ROWS, 128), F32),
            vmem((2 * ROWS, 128), F32),
            vmem((SEQ, 16, 128), BF),
            vmem((2, SEQ, 16, 128), BF),
            vmem((SEQ, 16, 128), BF),
            vmem((2, SEQ, 16, 128), BF),
            vmem((LG, NKEY, 128), BF),
            vmem((LG, VROWS, NKEY), BF),
            vmem((LG, 4 * PAIRS, 128), BF),
            vmem((2, SEQ, 4, 128), BF),
            pltpu.SemaphoreType.DMA((4,)),
            pltpu.SemaphoreType.DMA,
            pltpu.SemaphoreType.DMA,
            pltpu.SemaphoreType.DMA((2,)),
            pltpu.SemaphoreType.DMA((2,)),
            pltpu.SemaphoreType.DMA,
            pltpu.SemaphoreType.DMA,
            pltpu.SemaphoreType.DMA((2,)),
            pltpu.SemaphoreType.DMA((2,)),
            pltpu.SemaphoreType.REGULAR,
        ],
        compiler_params=pltpu.CompilerParams(
            collective_id=0, has_side_effects=True, vmem_limit_bytes=48 * 1024 * 1024
        ),
    )(patch_index, block_split, *large)
    cache, att, handed = pl.pallas_call(
        write_out,
        out_shape=[
            jax.ShapeDtypeStruct((LG, 2 * ROWS, 128), BF),
            jax.ShapeDtypeStruct((4 * PAIRS, 128), BF),
            jax.ShapeDtypeStruct((2, SEQ, 512), BF),
        ],
        in_specs=[pl.BlockSpec(memory_space=vmem)] * 4,
        out_specs=[pl.BlockSpec(memory_space=pltpu.HBM)] * 3,
        scratch_shapes=[
            vmem((PAIRS, 128), F32),
            vmem((2, SEQ, 512), BF),
            pltpu.SemaphoreType.DMA((6,)),
        ],
    )(*[pltpu.with_memory_space_constraint(part, vmem) for part in kept])
    cache = cache.reshape(LG, ROWS, 2, 128).transpose(0, 2, 1, 3).reshape(kv_cache.shape)
    att = att.reshape(2, PAIRS, 2, 128).transpose(0, 2, 1, 3).reshape(2, 2, 1, 2 * PAIRS * HD)
    return cache, att, handed.reshape(entering.shape)


def solution(mesh):
    in_specs = (
        P("section", None, None, None, "seq"),
        P("section", None, "seq", None, None),
        P("section", None, "seq", None, None),
        P("section", None, None, "seq"),
        P("section", None, None),
        P("section"),
        P("section"),
    )
    out_specs = (
        P("section", None, "seq", None, None),
        P("section", None, "seq", None),
        P("section", None, None, "seq"),
    )
    return jax.shard_map(
        on_device, mesh=mesh, in_specs=in_specs, out_specs=out_specs, check_vma=False
    )
```

```python
import math

import jax
import jax.numpy as jnp
from jax import lax
from jax.experimental import pallas as pl
from jax.experimental.pallas import tpu as pltpu
from jax.sharding import PartitionSpec as P

HD = 64
PATCHES = 4
TXT = 333
SEQ = 32
PAIRS = 128
ROWS = 512
STALE = 384
TROWS = 176
NKEY = STALE + TROWS
VROWS = 144
LG = 4
MESH = pl.DeviceIdType.MESH
BF = jnp.bfloat16
F32 = jnp.float32
FACTOR = HD ** (-0.5) * math.log2(math.e)


def far_first():
    hops = (0, 1, 2, 1)
    return sorted(range(1, SEQ), key=lambda flip: -(hops[flip // 8] + hops[flip // 2 % 4]))


def low_rows(shape):
    return lax.broadcasted_iota(jnp.int32, shape, len(shape) - 2) < 4


def split_layers(x):
    pieces = x.astype(F32).reshape(16, 2, 8, 128)
    even, odd = pieces[:, 0], pieces[:, 1]
    mask = low_rows(even.shape)
    first = jnp.where(mask, even, pltpu.roll(odd, 4, 1))
    second = jnp.where(mask, pltpu.roll(even, 4, 1), odd)
    return first.reshape(PAIRS, 128), second.reshape(PAIRS, 128)


def kernel(
    patch_s, split_s, gates_hbm, qkv_hbm, kv_hbm, text_hbm, ent_hbm,
    cache, att, recv_b, ent_v,
    gates_v, qkv_v, text_v, stage, tstage,
    send_q, send_kv, recv_q, recv_kv, keys, values, queries, send_b,
    load_sem, q_send, q_recv, kv_send, kv_recv, e_send, e_recv, b_send, b_recv, ready_sem,
):
    sections = lax.axis_size("section")
    sec = lax.axis_index("section")
    me = lax.axis_index("seq")
    after = lax.rem(sec + 1, sections)
    before = lax.rem(sec + sections - 1, sections)

    load_q = pltpu.make_async_copy(qkv_hbm.at[:, 0], qkv_v.at[:, 0], load_sem.at[0])
    own_kv = pl.ds(1, 2)
    load_own = pltpu.make_async_copy(qkv_hbm.at[:, own_kv], qkv_v.at[:, own_kv], load_sem.at[4])
    load_kv = pltpu.make_async_copy(kv_hbm, cache, load_sem.at[1])
    load_text = pltpu.make_async_copy(text_hbm, text_v, load_sem.at[2])
    load_gates = pltpu.make_async_copy(gates_hbm, gates_v, load_sem.at[3])
    load_q.start()
    load_own.start()

    barrier = pltpu.get_barrier_semaphore()
    for other in (after, before):
        pl.semaphore_signal(barrier, inc=1, device_id=(other, me), device_id_type=MESH)
    for flip in far_first():
        pl.semaphore_signal(
            barrier, inc=1, device_id=(sec, jnp.bitwise_xor(me, flip)), device_id_type=MESH
        )
    load_kv.start()
    load_text.start()
    load_gates.start()

    def arrange(half, parts):
        places = [(part, layer) for part in parts for layer in range(2)]
        size = 4 * len(places)
        for place, (part, layer) in enumerate(places):
            rows = qkv_v[layer * 2 + half, part].astype(F32)
            for at in range(4):
                stage[pl.ds(place * 4 + at, SEQ, stride=size), :] = (
                    rows[:, at * 128:(at + 1) * 128]
                )
        return stage[0:SEQ * size].reshape(SEQ, size, 128).astype(BF)

    load_q.wait()
    for half in range(2):
        send_q[half] = arrange(half, [0])
    pl.semaphore_wait(barrier, SEQ + 1)

    def q_copy(half, other):
        return pltpu.make_async_remote_copy(
            src_ref=send_q.at[half, other], dst_ref=recv_q.at[half, me],
            send_sem=q_send.at[half], recv_sem=q_recv.at[half],
            device_id=(sec, other), device_id_type=MESH,
        )

    def kv_copy(half, other):
        return pltpu.make_async_remote_copy(
            src_ref=send_kv.at[half, other], dst_ref=recv_kv.at[half, me],
            send_sem=kv_send.at[half], recv_sem=kv_recv.at[half],
            device_id=(sec, other), device_id_type=MESH,
        )

    def b_copy(half, other):
        return pltpu.make_async_remote_copy(
            src_ref=send_b.at[half, other], dst_ref=recv_b.at[half, me],
            send_sem=b_send.at[half], recv_sem=b_recv.at[half],
            device_id=(after, other), device_id_type=MESH,
        )

    for half in range(2):
        for flip in far_first():
            q_copy(half, jnp.bitwise_xor(me, flip)).start()
        pltpu.make_async_copy(send_q.at[half, me], recv_q.at[half, me], q_recv.at[half]).start()
    load_own.wait()
    for half in range(2):
        send_kv[half] = arrange(half, [1, 2])
        for flip in far_first():
            kv_copy(half, jnp.bitwise_xor(me, flip)).start()
        pltpu.make_async_copy(
            send_kv.at[half, me], recv_kv.at[half, me], kv_recv.at[half]
        ).start()
    pl.semaphore_signal(ready_sem, inc=1, device_id=(before, me), device_id_type=MESH)
    ent_copy = pltpu.make_async_remote_copy(
        src_ref=ent_hbm, dst_ref=ent_v, send_sem=e_send, recv_sem=e_recv,
        device_id=(after, me), device_id_type=MESH,
    )
    ent_copy.start()

    load_kv.wait()
    load_text.wait()
    load_gates.wait()
    slots = jnp.full((PAIRS, 128), patch_s[0], jnp.int32)
    counts = jnp.full((PAIRS, 128), split_s[0], jnp.int32)
    column = lax.broadcasted_iota(jnp.int32, (VROWS - 128, NKEY), 1)
    evens = lax.broadcasted_iota(jnp.int32, (VROWS - 128, NKEY), 0) < 8
    whole_pairs = STALE + TXT // 2
    counted = (column < whole_pairs) | ((column == whole_pairs) & evens)
    ones = jnp.where(counted, 1.0, 0.0).astype(BF)

    def prepare(lg, carry):
        tstage[...] = cache[lg].astype(F32)
        for at in range(PATCHES - 1):
            ahead = at < slots
            rows = pl.ds(at * PAIRS, PAIRS)
            here, later = at * 256, (at + 1) * 256
            keys[lg, rows, :] = jnp.where(
                ahead,
                tstage[pl.ds(here, PAIRS, stride=2), :],
                tstage[pl.ds(later, PAIRS, stride=2), :],
            ).astype(BF)
            values[lg, 0:128, rows] = jnp.where(
                ahead,
                tstage[pl.ds(here + 1, PAIRS, stride=2), :],
                tstage[pl.ds(later + 1, PAIRS, stride=2), :],
            ).T.astype(BF)
        for at in range(TXT // 2):
            tstage[2 * at:2 * at + 2, :] = text_v[lg, :, at * 128:(at + 1) * 128].astype(F32)
        last = text_v[lg, :, TXT // 2 * 128:TXT * HD].astype(F32)
        last = jnp.concatenate([last, last], axis=1)
        row = lax.broadcasted_iota(jnp.int32, (TROWS, 128), 0)
        lane = lax.broadcasted_iota(jnp.int32, (TROWS, 128), 1)
        whole = row < TXT // 2
        half = (row == TXT // 2) & (lane < HD)
        keys[lg, STALE:, :] = jnp.where(
            whole, tstage[pl.ds(0, TROWS, stride=2), :], last[0:1]
        ).astype(BF)
        end = jnp.where(half, last[1:2], 0.0)
        values[lg, 0:128, STALE:] = jnp.where(
            whole, tstage[pl.ds(1, TROWS, stride=2), :], end
        ).T.astype(BF)
        values[lg, 128:, :] = ones
        return carry

    lax.fori_loop(0, LG, prepare, 0)

    lanes = lax.broadcasted_iota(jnp.int32, (PAIRS, 128), 1) < HD

    def place_queries(half):
        pltpu.make_async_copy(recv_q.at[half], recv_q.at[half], q_recv.at[half]).wait()
        for layer, q in enumerate(split_layers(recv_q[half])):
            lg = layer * 2 + half
            turned = pltpu.roll(q, HD, 1)
            queries[lg, 0:128] = jnp.where(lanes, q, 0.0).astype(BF)
            queries[lg, 128:256] = jnp.where(lanes, turned, 0.0).astype(BF)
            queries[lg, 256:384] = jnp.where(lanes, 0.0, turned).astype(BF)
            queries[lg, 384:512] = jnp.where(lanes, 0.0, q).astype(BF)

    def scores_of(lg, k):
        s = lax.dot_general(k, queries[lg], (((1,), (1,)), ((), ())), preferred_element_type=F32)
        best = jnp.max(s, axis=0, keepdims=True)
        return s, jnp.maximum(best[:, 0:256], best[:, 256:512])

    def twice(x):
        return jnp.concatenate([x, x], axis=1)

    old, partial = [None] * LG, [None] * LG
    for lg in (0, 2, 1, 3):
        if lg < 2:
            place_queries(lg)
        s, best = scores_of(lg, keys[lg])
        w = jnp.exp2((s - twice(best)) * FACTOR).astype(BF)
        old[lg] = best
        partial[lg] = jnp.dot(values[lg], w, preferred_element_type=F32)

    mine = lax.broadcasted_iota(jnp.int32, (2, SEQ), 1) == me
    gate = [
        jnp.sum(jnp.where(mine, gates_v[layer], 0.0), axis=1, keepdims=True) for layer in range(2)
    ]

    def attend_fresh(lg, k, v):
        s, best = scores_of(lg, k.astype(BF))
        best = jnp.maximum(old[lg], best)
        w = jnp.exp2((s - twice(best)) * FACTOR).astype(BF)
        v = jnp.concatenate([v.T.astype(BF), jnp.ones((VROWS - 128, PAIRS), BF)], axis=0)
        scale = jnp.exp2((old[lg] - best) * FACTOR)
        total = jnp.dot(v, w, preferred_element_type=F32) + partial[lg] * twice(scale)

        def joined(at, low, high, size):
            cols = slice(at * 128, at * 128 + 128)
            cols2 = slice(at * 128 + 256, at * 128 + 384)
            return total[low:low + size, cols] + total[high:high + size, cols2]

        out = jnp.concatenate(
            [joined(at, 0, 64, 64) / joined(at, 128, 136, 8)[0:1] for at in range(2)], axis=0
        ).T
        return jnp.where(lg // 2 < counts, out, 0.0).astype(BF).astype(F32)

    fresh, attended = [None] * LG, [None] * LG
    for half in range(2):
        pltpu.make_async_copy(recv_kv.at[half], recv_kv.at[half], kv_recv.at[half]).wait()
        pieces = split_layers(recv_kv[half, :, 0:8]) + split_layers(recv_kv[half, :, 8:16])
        branch = None
        for layer in range(2):
            lg = layer * 2 + half
            fresh[lg] = pieces[layer], pieces[2 + layer]
            attended[lg] = attend_fresh(lg, *fresh[lg])
            gated = gate[layer][half:half + 1] * attended[lg]
            branch = gated if branch is None else branch + gated
        send_b[half] = branch.reshape(SEQ, 4, 128).astype(BF)
        if half == 0:
            pl.semaphore_wait(ready_sem, 1)
        for flip in far_first() + [0]:
            b_copy(half, jnp.bitwise_xor(me, flip)).start()

    for lg in range(LG):
        layer, half = lg // 2, lg % 2
        tstage[pl.ds(lg * 256, PAIRS, stride=2), :] = fresh[lg][0]
        tstage[pl.ds(lg * 256 + 1, PAIRS, stride=2), :] = fresh[lg][1]
        for at in range(PATCHES * 2):
            here = (layer < counts) & (slots == at // 2)
            rows = pl.ds(at * 128, 128)
            new = tstage[pl.ds(lg * 256 + at % 2 * 128, 128), :]
            cache[lg, rows, :] = jnp.where(here, new, cache[lg, rows, :].astype(F32)).astype(BF)
        stage[pl.ds(layer * 256 + half, PAIRS, stride=2), :] = attended[lg]
    att[...] = stage[...].astype(BF)

    rest = pl.ds(0, SEQ - 1)
    for half in range(2):
        part = send_q.at[half, rest]
        pltpu.make_async_copy(part, part, q_send.at[half]).wait()
        part = send_kv.at[half, rest]
        pltpu.make_async_copy(part, part, kv_send.at[half]).wait()
    ent_copy.wait()
    for half in range(2):
        pltpu.make_async_copy(send_b.at[half], send_b.at[half], b_send.at[half]).wait()
        pltpu.make_async_copy(recv_b.at[half], recv_b.at[half], b_recv.at[half]).wait()


def write_out(
    cache, att, recv_b, ent_v, cache_hbm, att_hbm, hand_hbm, moved, hand, sem
):
    copies = [pltpu.make_async_copy(cache.at[lg], cache_hbm.at[lg], sem.at[lg]) for lg in range(LG)]
    copies.append(pltpu.make_async_copy(att, att_hbm, sem.at[4]))
    for copy in copies:
        copy.start()
    for half in range(2):
        moved[...] = recv_b[half].astype(F32).reshape(PAIRS, 128)
        for at in range(4):
            cols = pl.ds(at * 128, 128)
            branch = moved[pl.ds(at, SEQ, stride=4), :]
            hand[half, :, cols] = (ent_v[half, :, cols].astype(F32) + branch).astype(BF)
    copies.append(pltpu.make_async_copy(hand, hand_hbm, sem.at[5]))
    copies[-1].start()
    for copy in copies:
        copy.wait()


def on_device(patch_qkv, kv_cache, text_kv, entering, gates, block_split, patch_index):
    qkv = jnp.transpose(patch_qkv, (0, 1, 3, 2, 4)).reshape(LG, 3, SEQ, 512)
    kv = kv_cache.reshape(LG, 2, ROWS, 128).transpose(0, 2, 1, 3).reshape(LG, 2 * ROWS, 128)
    text = text_kv.reshape(LG, 2, TXT * HD)
    ent = entering.reshape(2, SEQ, 512)
    large = [
        pltpu.with_memory_space_constraint(operand, pltpu.HBM)
        for operand in (gates, qkv, kv, text, ent)
    ]
    vmem = pltpu.VMEM
    kept = pl.pallas_call(
        kernel,
        out_shape=[
            vmem((LG, 2 * ROWS, 128), BF),
            vmem((4 * PAIRS, 128), BF),
            vmem((2, SEQ, 4, 128), BF),
            vmem((2, SEQ, 512), BF),
        ],
        in_specs=[pl.BlockSpec(memory_space=pltpu.SMEM)] * 2
        + [pl.BlockSpec(memory_space=pltpu.HBM)] * 5,
        out_specs=[pl.BlockSpec(memory_space=vmem)] * 4,
        scratch_shapes=[
            vmem((2, 2, SEQ), F32),
            vmem((LG, 3, SEQ, 512), BF),
            vmem((LG, 2, TXT * HD), BF),
            vmem((ROWS, 128), F32),
            vmem((2 * ROWS, 128), F32),
            vmem((2, SEQ, 8, 128), BF),
            vmem((2, SEQ, 16, 128), BF),
            vmem((2, SEQ, 8, 128), BF),
            vmem((2, SEQ, 16, 128), BF),
            vmem((LG, NKEY, 128), BF),
            vmem((LG, VROWS, NKEY), BF),
            vmem((LG, 4 * PAIRS, 128), BF),
            vmem((2, SEQ, 4, 128), BF),
            pltpu.SemaphoreType.DMA((5,)),
            pltpu.SemaphoreType.DMA((2,)),
            pltpu.SemaphoreType.DMA((2,)),
            pltpu.SemaphoreType.DMA((2,)),
            pltpu.SemaphoreType.DMA((2,)),
            pltpu.SemaphoreType.DMA,
            pltpu.SemaphoreType.DMA,
            pltpu.SemaphoreType.DMA((2,)),
            pltpu.SemaphoreType.DMA((2,)),
            pltpu.SemaphoreType.REGULAR,
        ],
        compiler_params=pltpu.CompilerParams(
            collective_id=0, has_side_effects=True, vmem_limit_bytes=48 * 1024 * 1024
        ),
    )(patch_index, block_split, *large)
    cache, att, handed = pl.pallas_call(
        write_out,
        out_shape=[
            jax.ShapeDtypeStruct((LG, 2 * ROWS, 128), BF),
            jax.ShapeDtypeStruct((4 * PAIRS, 128), BF),
            jax.ShapeDtypeStruct((2, SEQ, 512), BF),
        ],
        in_specs=[pl.BlockSpec(memory_space=vmem)] * 4,
        out_specs=[pl.BlockSpec(memory_space=pltpu.HBM)] * 3,
        scratch_shapes=[
            vmem((PAIRS, 128), F32),
            vmem((2, SEQ, 512), BF),
            pltpu.SemaphoreType.DMA((6,)),
        ],
    )(*[pltpu.with_memory_space_constraint(part, vmem) for part in kept])
    cache = cache.reshape(LG, ROWS, 2, 128).transpose(0, 2, 1, 3).reshape(kv_cache.shape)
    att = att.reshape(2, PAIRS, 2, 128).transpose(0, 2, 1, 3).reshape(2, 2, 1, 2 * PAIRS * HD)
    return cache, att, handed.reshape(entering.shape)


def solution(mesh):
    in_specs = (
        P("section", None, None, None, "seq"),
        P("section", None, "seq", None, None),
        P("section", None, "seq", None, None),
        P("section", None, None, "seq"),
        P("section", None, None),
        P("section"),
        P("section"),
    )
    out_specs = (
        P("section", None, "seq", None, None),
        P("section", None, "seq", None),
        P("section", None, None, "seq"),
    )
    return jax.shard_map(
        on_device, mesh=mesh, in_specs=in_specs, out_specs=out_specs, check_vma=False
    )
```

```python
import math

import jax
import jax.numpy as jnp
from jax import lax
from jax.experimental import pallas as pl
from jax.experimental.pallas import tpu as pltpu
from jax.sharding import PartitionSpec as P

HD = 64
PATCHES = 4
TXT = 333
SEQ = 32
PAIRS = 128
ROWS = 512
STALE = 384
TROWS = 176
NKEY = STALE + TROWS
VROWS = 144
LG = 4
MESH = pl.DeviceIdType.MESH
BF = jnp.bfloat16
F32 = jnp.float32
FACTOR = HD ** (-0.5) * math.log2(math.e)


def far_first():
    hops = (0, 1, 2, 1)
    return sorted(range(1, SEQ), key=lambda flip: -(hops[flip // 8] + hops[flip // 2 % 4]))


def low_rows(shape):
    return lax.broadcasted_iota(jnp.int32, shape, len(shape) - 2) < 4


def split_layers(x):
    pieces = x.astype(F32).reshape(16, 2, 8, 128)
    even, odd = pieces[:, 0], pieces[:, 1]
    mask = low_rows(even.shape)
    first = jnp.where(mask, even, pltpu.roll(odd, 4, 1))
    second = jnp.where(mask, pltpu.roll(even, 4, 1), odd)
    return first.reshape(PAIRS, 128), second.reshape(PAIRS, 128)


def kernel(
    patch_s, split_s, gates_hbm, qkv_hbm, kv_hbm, text_hbm, ent_hbm,
    cache, att, recv_b, ent_v,
    gates_v, qkv_v, text_v, stage, tstage,
    send_q, send_kv, recv_q, recv_kv, keys, values, queries, send_b,
    load_sem, q_send, q_recv, kv_send, kv_recv, e_send, e_recv, b_send, b_recv, ready_sem,
):
    sections = lax.axis_size("section")
    sec = lax.axis_index("section")
    me = lax.axis_index("seq")
    after = lax.rem(sec + 1, sections)
    before = lax.rem(sec + sections - 1, sections)

    load_q = pltpu.make_async_copy(qkv_hbm.at[:, 0], qkv_v.at[:, 0], load_sem.at[0])
    own_kv = pl.ds(1, 2)
    load_own = pltpu.make_async_copy(qkv_hbm.at[:, own_kv], qkv_v.at[:, own_kv], load_sem.at[4])
    load_kv = pltpu.make_async_copy(kv_hbm, cache, load_sem.at[1])
    load_text = pltpu.make_async_copy(text_hbm, text_v, load_sem.at[2])
    load_gates = pltpu.make_async_copy(gates_hbm, gates_v, load_sem.at[3])
    load_q.start()
    load_own.start()

    barrier = pltpu.get_barrier_semaphore()
    for other in (after, before):
        pl.semaphore_signal(barrier, inc=1, device_id=(other, me), device_id_type=MESH)
    for flip in far_first():
        pl.semaphore_signal(
            barrier, inc=1, device_id=(sec, jnp.bitwise_xor(me, flip)), device_id_type=MESH
        )
    load_kv.start()
    load_text.start()
    load_gates.start()

    def arrange(half, parts):
        places = [(part, layer) for part in parts for layer in range(2)]
        size = 4 * len(places)
        for place, (part, layer) in enumerate(places):
            rows = qkv_v[layer * 2 + half, part].astype(F32)
            for at in range(4):
                stage[pl.ds(place * 4 + at, SEQ, stride=size), :] = (
                    rows[:, at * 128:(at + 1) * 128]
                )
        return stage[0:SEQ * size].reshape(SEQ, size, 128).astype(BF)

    load_q.wait()
    for half in range(2):
        send_q[half] = arrange(half, [0])
    pl.semaphore_wait(barrier, SEQ + 1)

    def q_copy(half, other):
        return pltpu.make_async_remote_copy(
            src_ref=send_q.at[half, other], dst_ref=recv_q.at[half, me],
            send_sem=q_send.at[half], recv_sem=q_recv.at[half],
            device_id=(sec, other), device_id_type=MESH,
        )

    def kv_copy(half, other):
        return pltpu.make_async_remote_copy(
            src_ref=send_kv.at[half, other], dst_ref=recv_kv.at[half, me],
            send_sem=kv_send.at[half], recv_sem=kv_recv.at[half],
            device_id=(sec, other), device_id_type=MESH,
        )

    def b_copy(half, other):
        return pltpu.make_async_remote_copy(
            src_ref=send_b.at[half, other], dst_ref=recv_b.at[half, me],
            send_sem=b_send.at[half], recv_sem=b_recv.at[half],
            device_id=(after, other), device_id_type=MESH,
        )

    for half in range(2):
        for flip in far_first():
            q_copy(half, jnp.bitwise_xor(me, flip)).start()
        pltpu.make_async_copy(send_q.at[half, me], recv_q.at[half, me], q_recv.at[half]).start()
    load_own.wait()
    for half in range(2):
        send_kv[half] = arrange(half, [1, 2])
        for flip in far_first():
            kv_copy(half, jnp.bitwise_xor(me, flip)).start()
        pltpu.make_async_copy(
            send_kv.at[half, me], recv_kv.at[half, me], kv_recv.at[half]
        ).start()
    pl.semaphore_signal(ready_sem, inc=1, device_id=(before, me), device_id_type=MESH)
    ent_copy = pltpu.make_async_remote_copy(
        src_ref=ent_hbm, dst_ref=ent_v, send_sem=e_send, recv_sem=e_recv,
        device_id=(after, me), device_id_type=MESH,
    )
    ent_copy.start()

    load_kv.wait()
    load_text.wait()
    load_gates.wait()
    slots = jnp.full((PAIRS, 128), patch_s[0], jnp.int32)
    counts = jnp.full((PAIRS, 128), split_s[0], jnp.int32)
    column = lax.broadcasted_iota(jnp.int32, (VROWS - 128, NKEY), 1)
    evens = lax.broadcasted_iota(jnp.int32, (VROWS - 128, NKEY), 0) < 8
    whole_pairs = STALE + TXT // 2
    counted = (column < whole_pairs) | ((column == whole_pairs) & evens)
    ones = jnp.where(counted, 1.0, 0.0).astype(BF)

    def prepare(lg, carry):
        tstage[...] = cache[lg].astype(F32)
        for at in range(PATCHES - 1):
            ahead = at < slots
            rows = pl.ds(at * PAIRS, PAIRS)
            here, later = at * 256, (at + 1) * 256
            keys[lg, rows, :] = jnp.where(
                ahead,
                tstage[pl.ds(here, PAIRS, stride=2), :],
                tstage[pl.ds(later, PAIRS, stride=2), :],
            ).astype(BF)
            values[lg, 0:128, rows] = jnp.where(
                ahead,
                tstage[pl.ds(here + 1, PAIRS, stride=2), :],
                tstage[pl.ds(later + 1, PAIRS, stride=2), :],
            ).T.astype(BF)
        for at in range(TXT // 2):
            tstage[2 * at:2 * at + 2, :] = text_v[lg, :, at * 128:(at + 1) * 128].astype(F32)
        last = text_v[lg, :, TXT // 2 * 128:TXT * HD].astype(F32)
        last = jnp.concatenate([last, last], axis=1)
        row = lax.broadcasted_iota(jnp.int32, (TROWS, 128), 0)
        lane = lax.broadcasted_iota(jnp.int32, (TROWS, 128), 1)
        whole = row < TXT // 2
        half = (row == TXT // 2) & (lane < HD)
        keys[lg, STALE:, :] = jnp.where(
            whole, tstage[pl.ds(0, TROWS, stride=2), :], last[0:1]
        ).astype(BF)
        end = jnp.where(half, last[1:2], 0.0)
        values[lg, 0:128, STALE:] = jnp.where(
            whole, tstage[pl.ds(1, TROWS, stride=2), :], end
        ).T.astype(BF)
        values[lg, 128:, :] = ones
        return carry

    lax.fori_loop(0, LG, prepare, 0)

    lanes = lax.broadcasted_iota(jnp.int32, (PAIRS, 128), 1) < HD

    def place_queries(half):
        pltpu.make_async_copy(recv_q.at[half], recv_q.at[half], q_recv.at[half]).wait()
        for layer, q in enumerate(split_layers(recv_q[half])):
            lg = layer * 2 + half
            turned = pltpu.roll(q, HD, 1)
            queries[lg, 0:128] = jnp.where(lanes, q, 0.0).astype(BF)
            queries[lg, 128:256] = jnp.where(lanes, turned, 0.0).astype(BF)
            queries[lg, 256:384] = jnp.where(lanes, 0.0, turned).astype(BF)
            queries[lg, 384:512] = jnp.where(lanes, 0.0, q).astype(BF)

    def scores_of(lg, k):
        s = lax.dot_general(k, queries[lg], (((1,), (1,)), ((), ())), preferred_element_type=F32)
        best = jnp.max(s, axis=0, keepdims=True)
        return s, jnp.maximum(best[:, 0:256], best[:, 256:512])

    def twice(x):
        return jnp.concatenate([x, x], axis=1)

    old, partial = [None] * LG, [None] * LG
    for half in range(2):
        place_queries(half)
        pair = [scores_of(lg, keys[lg]) for lg in (half, 2 + half)]
        for lg, (s, best) in zip((half, 2 + half), pair):
            w = jnp.exp2((s - twice(best)) * FACTOR).astype(BF)
            old[lg] = best
            partial[lg] = jnp.dot(values[lg], w, preferred_element_type=F32)

    mine = lax.broadcasted_iota(jnp.int32, (2, SEQ), 1) == me
    gate = [
        jnp.sum(jnp.where(mine, gates_v[layer], 0.0), axis=1, keepdims=True) for layer in range(2)
    ]

    def attend_fresh(lg, k, v):
        s, best = scores_of(lg, k.astype(BF))
        best = jnp.maximum(old[lg], best)
        w = jnp.exp2((s - twice(best)) * FACTOR).astype(BF)
        v = jnp.concatenate([v.T.astype(BF), jnp.ones((VROWS - 128, PAIRS), BF)], axis=0)
        scale = jnp.exp2((old[lg] - best) * FACTOR)
        total = jnp.dot(v, w, preferred_element_type=F32) + partial[lg] * twice(scale)

        def joined(at, low, high, size):
            cols = slice(at * 128, at * 128 + 128)
            cols2 = slice(at * 128 + 256, at * 128 + 384)
            return total[low:low + size, cols] + total[high:high + size, cols2]

        out = jnp.concatenate(
            [joined(at, 0, 64, 64) / joined(at, 128, 136, 8)[0:1] for at in range(2)], axis=0
        ).T
        return jnp.where(lg // 2 < counts, out, 0.0).astype(BF).astype(F32)

    fresh, attended = [None] * LG, [None] * LG
    for half in range(2):
        pltpu.make_async_copy(recv_kv.at[half], recv_kv.at[half], kv_recv.at[half]).wait()
        pieces = split_layers(recv_kv[half, :, 0:8]) + split_layers(recv_kv[half, :, 8:16])
        branch = None
        for layer in range(2):
            lg = layer * 2 + half
            fresh[lg] = pieces[layer], pieces[2 + layer]
            attended[lg] = attend_fresh(lg, *fresh[lg])
            gated = gate[layer][half:half + 1] * attended[lg]
            branch = gated if branch is None else branch + gated
        send_b[half] = branch.reshape(SEQ, 4, 128).astype(BF)
        if half == 0:
            pl.semaphore_wait(ready_sem, 1)
        for flip in far_first() + [0]:
            b_copy(half, jnp.bitwise_xor(me, flip)).start()

    for lg in range(LG):
        layer, half = lg // 2, lg % 2
        tstage[pl.ds(lg * 256, PAIRS, stride=2), :] = fresh[lg][0]
        tstage[pl.ds(lg * 256 + 1, PAIRS, stride=2), :] = fresh[lg][1]
        for at in range(PATCHES * 2):
            here = (layer < counts) & (slots == at // 2)
            rows = pl.ds(at * 128, 128)
            new = tstage[pl.ds(lg * 256 + at % 2 * 128, 128), :]
            cache[lg, rows, :] = jnp.where(here, new, cache[lg, rows, :].astype(F32)).astype(BF)
        stage[pl.ds(layer * 256 + half, PAIRS, stride=2), :] = attended[lg]
    att[...] = stage[...].astype(BF)

    rest = pl.ds(0, SEQ - 1)
    for half in range(2):
        part = send_q.at[half, rest]
        pltpu.make_async_copy(part, part, q_send.at[half]).wait()
        part = send_kv.at[half, rest]
        pltpu.make_async_copy(part, part, kv_send.at[half]).wait()
    ent_copy.wait()
    for half in range(2):
        pltpu.make_async_copy(send_b.at[half], send_b.at[half], b_send.at[half]).wait()
        pltpu.make_async_copy(recv_b.at[half], recv_b.at[half], b_recv.at[half]).wait()


def write_out(
    cache, att, recv_b, ent_v, cache_hbm, att_hbm, hand_hbm, moved, hand, sem
):
    copies = [pltpu.make_async_copy(cache.at[lg], cache_hbm.at[lg], sem.at[lg]) for lg in range(LG)]
    copies.append(pltpu.make_async_copy(att, att_hbm, sem.at[4]))
    for copy in copies:
        copy.start()
    for half in range(2):
        moved[...] = recv_b[half].astype(F32).reshape(PAIRS, 128)
        for at in range(4):
            cols = pl.ds(at * 128, 128)
            branch = moved[pl.ds(at, SEQ, stride=4), :]
            hand[half, :, cols] = (ent_v[half, :, cols].astype(F32) + branch).astype(BF)
    copies.append(pltpu.make_async_copy(hand, hand_hbm, sem.at[5]))
    copies[-1].start()
    for copy in copies:
        copy.wait()


def on_device(patch_qkv, kv_cache, text_kv, entering, gates, block_split, patch_index):
    qkv = jnp.transpose(patch_qkv, (0, 1, 3, 2, 4)).reshape(LG, 3, SEQ, 512)
    kv = kv_cache.reshape(LG, 2, ROWS, 128).transpose(0, 2, 1, 3).reshape(LG, 2 * ROWS, 128)
    text = text_kv.reshape(LG, 2, TXT * HD)
    ent = entering.reshape(2, SEQ, 512)
    large = [
        pltpu.with_memory_space_constraint(operand, pltpu.HBM)
        for operand in (gates, qkv, kv, text, ent)
    ]
    vmem = pltpu.VMEM
    kept = pl.pallas_call(
        kernel,
        out_shape=[
            vmem((LG, 2 * ROWS, 128), BF),
            vmem((4 * PAIRS, 128), BF),
            vmem((2, SEQ, 4, 128), BF),
            vmem((2, SEQ, 512), BF),
        ],
        in_specs=[pl.BlockSpec(memory_space=pltpu.SMEM)] * 2
        + [pl.BlockSpec(memory_space=pltpu.HBM)] * 5,
        out_specs=[pl.BlockSpec(memory_space=vmem)] * 4,
        scratch_shapes=[
            vmem((2, 2, SEQ), F32),
            vmem((LG, 3, SEQ, 512), BF),
            vmem((LG, 2, TXT * HD), BF),
            vmem((ROWS, 128), F32),
            vmem((2 * ROWS, 128), F32),
            vmem((2, SEQ, 8, 128), BF),
            vmem((2, SEQ, 16, 128), BF),
            vmem((2, SEQ, 8, 128), BF),
            vmem((2, SEQ, 16, 128), BF),
            vmem((LG, NKEY, 128), BF),
            vmem((LG, VROWS, NKEY), BF),
            vmem((LG, 4 * PAIRS, 128), BF),
            vmem((2, SEQ, 4, 128), BF),
            pltpu.SemaphoreType.DMA((5,)),
            pltpu.SemaphoreType.DMA((2,)),
            pltpu.SemaphoreType.DMA((2,)),
            pltpu.SemaphoreType.DMA((2,)),
            pltpu.SemaphoreType.DMA((2,)),
            pltpu.SemaphoreType.DMA,
            pltpu.SemaphoreType.DMA,
            pltpu.SemaphoreType.DMA((2,)),
            pltpu.SemaphoreType.DMA((2,)),
            pltpu.SemaphoreType.REGULAR,
        ],
        compiler_params=pltpu.CompilerParams(
            collective_id=0, has_side_effects=True, vmem_limit_bytes=48 * 1024 * 1024
        ),
    )(patch_index, block_split, *large)
    cache, att, handed = pl.pallas_call(
        write_out,
        out_shape=[
            jax.ShapeDtypeStruct((LG, 2 * ROWS, 128), BF),
            jax.ShapeDtypeStruct((4 * PAIRS, 128), BF),
            jax.ShapeDtypeStruct((2, SEQ, 512), BF),
        ],
        in_specs=[pl.BlockSpec(memory_space=vmem)] * 4,
        out_specs=[pl.BlockSpec(memory_space=pltpu.HBM)] * 3,
        scratch_shapes=[
            vmem((PAIRS, 128), F32),
            vmem((2, SEQ, 512), BF),
            pltpu.SemaphoreType.DMA((6,)),
        ],
    )(*[pltpu.with_memory_space_constraint(part, vmem) for part in kept])
    cache = cache.reshape(LG, ROWS, 2, 128).transpose(0, 2, 1, 3).reshape(kv_cache.shape)
    att = att.reshape(2, PAIRS, 2, 128).transpose(0, 2, 1, 3).reshape(2, 2, 1, 2 * PAIRS * HD)
    return cache, att, handed.reshape(entering.shape)


def solution(mesh):
    in_specs = (
        P("section", None, None, None, "seq"),
        P("section", None, "seq", None, None),
        P("section", None, "seq", None, None),
        P("section", None, None, "seq"),
        P("section", None, None),
        P("section"),
        P("section"),
    )
    out_specs = (
        P("section", None, "seq", None, None),
        P("section", None, "seq", None),
        P("section", None, None, "seq"),
    )
    return jax.shard_map(
        on_device, mesh=mesh, in_specs=in_specs, out_specs=out_specs, check_vma=False
    )
```
